32 devices in a mesh: depth: 4 (over z), freq: 8 (over y, x, core).
Axes of the slice: x: 2, y: 2, z: 4, core: 2. Of those that a mesh axis runs over, the one named last changes fastest.
Arguments:
- source: float32 [8, 2, 256, 256], P('freq'), may hold values from -6 to 6
- receiver: float32 [8, 2, 256, 256], P('freq'), may hold values from -6 to 6
- classes: int32 [4, 256, 256], P('depth'), may hold values from 0 to 15
- coef_table: float32 [16, 8, 2, 6], replicated, may hold values from -2 to 2, as said below
- freq_list: int32 [8], P('freq'), may hold values from 0 to 7, each once
Outputs:
- image: float32 [256, 4, 8, 256], P('freq', 'depth')
The draws below stay inside these ranges and needn't reach their ends.
Inputs may be any that keep to these rules, and one draw needn't show every extreme that they name: `coef_table`: every entry lies within the stated bounds.
All inputs are finite; a program needn't handle non-finite values.
Results may differ from the reference program's by a relative error of at most 0.00011.
Values sent between devices are 32-bit elements; how exact they have to be, the bound alone decides.
A program may use at most 64 MiB of HBM per device.

```python
import math
import jax
import jax.numpy as jnp

NX = 256
NY = 256
H = 8
K = 6
NCLASS = 16
F = 8
Z = 4


def draw_table(key, part):
    first, second, third = jax.random.split(jax.random.fold_in(key, 11), 3)
    slowness = jnp.exp(jax.random.uniform(first, (NCLASS,), jnp.float32, math.log(0.5), math.log(1.6)))
    omega = jax.random.uniform(second, (F,), jnp.float32, 0.3, 1.6)
    ratio = jax.random.uniform(third, (), jnp.float32, 0.8, 1.2)
    bound = slowness[:, None] * omega[None, :]
    nodes = 64
    angle = math.pi * (jnp.arange(nodes, dtype=jnp.float32) + 0.5) / nodes
    gap = angle[None, None, :] ** 2 - bound[:, :, None] ** 2
    phase = ratio * jnp.sqrt(jnp.maximum(-gap, 0.0))
    decay = jnp.exp(-ratio * jnp.sqrt(jnp.maximum(gap, 0.0)))
    value_real = jnp.where(gap < 0.0, jnp.cos(phase), decay)
    value_imag = jnp.where(gap < 0.0, jnp.sin(phase), 0.0)
    orders = jnp.arange(K, dtype=jnp.float32)
    basis = jnp.cos(orders[:, None] * angle[None, :])
    weights = jnp.where(orders == 0.0, 1.0, 2.0) / nodes
    coef_real = jnp.einsum('cgn,kn->cgk', value_real, basis) * weights
    coef_imag = jnp.einsum('cgn,kn->cgk', value_imag, basis) * weights
    fine = jnp.linspace(0.0, math.pi, 257)
    fine_basis = jnp.cos(orders[:, None] * fine[None, :])
    poly_real = jnp.einsum('cgk,kn->cgn', coef_real, fine_basis)
    poly_imag = jnp.einsum('cgk,kn->cgn', coef_imag, fine_basis)
    largest = jnp.max(jnp.sqrt(poly_real ** 2 + poly_imag ** 2 + 1e-12), axis=2)
    factor = 0.98 / largest
    table = jnp.stack([coef_real * factor[:, :, None], coef_imag * factor[:, :, None]], axis=2)
    return table.astype(jnp.float32)


def draw_coef_table(key, part):
    return draw_table(key, part)


def set_ends(values, stream_key, low, high):
    longest = values.shape.index(max(values.shape))
    spots = []
    for shift in (0, 1):
        where = [jax.random.randint(jax.random.fold_in(stream_key, axis), (), 0, length) for axis, length in enumerate(values.shape)]
        where[longest] = (where[longest] + shift) % values.shape[longest]
        spots.append(tuple(where))
    return values.at[spots[0]].set(low).at[spots[1]].set(high)


def strengthened(drawn, key, source, target, shards_of, factor):
    owner, partner = [(jnp.arange(drawn.shape[dim]) // (drawn.shape[dim] // shards_of)).reshape([-1 if axis == dim else 1 for axis in range(drawn.ndim)]) for dim in (source, target)]
    chosen = jax.random.permutation(key, shards_of)[partner]
    strong = (owner == chosen) | (owner == (partner + shards_of // 2) % shards_of)
    return jnp.where(strong, factor * drawn, drawn)


def levels(stream_key, shape, pieces, low, high):
    level = 1.0
    for position, parts in pieces:
        heights = jax.random.uniform(jax.random.fold_in(jax.random.fold_in(stream_key, 6), position), (parts,), jnp.float32, low / len(pieces), high / len(pieces))
        level = level * jnp.repeat(jnp.exp(heights), shape[position] // parts).reshape((-1,) + (1,) * (len(shape) - 1 - position))
    return level


def gaussian(stream_key, shape, scale, limit, cuts=(), kind=jnp.bfloat16):
    result = jax.random.normal(stream_key, shape, jnp.float32) * scale
    if len(cuts) > 0:
        result = levels(stream_key, shape, cuts, -0.22, 0.18) * result
    return jnp.clip(result, min=-limit, max=limit).astype(kind)


def bell_draw_with(own_key, dims, deviation, most, cuts, heavy, kind=jnp.bfloat16):
    result = deviation * jax.random.normal(own_key, dims, jnp.float32)
    if cuts:
        result = result * levels(own_key, dims, cuts, -0.22, 0.18)
    return jnp.clip(strengthened(result, jax.random.fold_in(own_key, 3), *heavy), -most, most).astype(kind)


def setup_inputs(seed: int = 0) -> dict:
    key_list = jax.random.split(jax.random.key(seed), 6)
    return {
        "source": gaussian(key_list[0], (F, 2, NX, NY), 1.0, 6.0, ((0, 8),), jnp.float32),
        "receiver": bell_draw_with(key_list[1], (F, 2, NX, NY), 1.0, 6.0, ((0, 8),), (0, 2, 8, 2.0), jnp.float32),
        "classes": set_ends(jax.random.randint(key_list[2], (Z, NX, NY), 0, NCLASS), jax.random.fold_in(key_list[2], 1), 0, NCLASS - 1).astype(jnp.int32),
        "coef_table": draw_coef_table(jax.random.fold_in(key_list[5], 71), 0),
        "freq_list": jax.random.permutation(key_list[4], F).astype(jnp.int32),
    }


def mcclellan(field):
    widths = [(0, 0)] * (field.ndim - 2) + [(1, 1), (1, 1)]
    padded = jnp.pad(field, widths)
    axial_sum = padded[..., 2:, 1:-1] + padded[..., :-2, 1:-1] + padded[..., 1:-1, 2:] + padded[..., 1:-1, :-2]
    corner_sum = padded[..., 2:, 2:] + padded[..., 2:, :-2] + padded[..., :-2, 2:] + padded[..., :-2, :-2]
    return -0.5 * field + 0.25 * axial_sum + 0.125 * corner_sum


def extrapolate(fields, coeffs):
    terms = coeffs.shape[3]
    earlier = fields
    current = mcclellan(fields)
    total_real = coeffs[:, :, 0, 0] * earlier[:, :, 0] - coeffs[:, :, 1, 0] * earlier[:, :, 1]
    total_imag = coeffs[:, :, 0, 0] * earlier[:, :, 1] + coeffs[:, :, 1, 0] * earlier[:, :, 0]
    for term_no in range(1, terms):
        total_real = total_real + coeffs[:, :, 0, term_no] * current[:, :, 0] - coeffs[:, :, 1, term_no] * current[:, :, 1]
        total_imag = total_imag + coeffs[:, :, 0, term_no] * current[:, :, 1] + coeffs[:, :, 1, term_no] * current[:, :, 0]
        if term_no + 1 < terms:
            following = 2.0 * mcclellan(current) - earlier
            earlier, current = current, following
    return jnp.stack([total_real, total_imag], axis=2)


def reference(source, receiver, classes, coef_table, freq_list):
    chosen = jnp.take(coef_table, freq_list, axis=1)
    chosen = jnp.transpose(chosen, (1, 2, 3, 0))
    imag_sign = jnp.array([1.0, -1.0], dtype=chosen.dtype)
    both_tables = jnp.stack([chosen * imag_sign[None, :, None, None], chosen])
    fields = jnp.stack([source, receiver])
    margin = H // 2
    scaling = F ** -0.5
    per_level = []
    for level in range(Z):
        coeffs = jnp.take(both_tables, classes[level], axis=4)
        fields = extrapolate(fields, coeffs)
        padded = jnp.pad(fields, [(0, 0), (0, 0), (0, 0), (margin, margin), (0, 0)])
        offsets = []
        for offset_no in range(H):
            shift_x = offset_no - margin
            src_part = padded[0, :, :, margin - shift_x:margin - shift_x + NX]
            rec_part = padded[1, :, :, margin + shift_x:margin + shift_x + NX]
            offsets.append(jnp.sum(src_part * rec_part, axis=(0, 1)))
        per_level.append(jnp.stack(offsets, axis=1))
    return jnp.stack(per_level, axis=1) * scaling
```

```python
import functools

import jax
import jax.numpy as jnp
from jax import lax
from jax.experimental import pallas as pl
from jax.experimental.pallas import tpu as pltpu
from jax.sharding import PartitionSpec as P

H = 8
LANES = 128
SUB = 8


def flip_rows(v, sub):
    v = pltpu.roll(v, 4, 0)
    v = jnp.where((sub & 2) == 0, pltpu.roll(v, 6, 0), pltpu.roll(v, 2, 0))
    return jnp.where((sub & 1) == 0, pltpu.roll(v, 7, 0), pltpu.roll(v, 1, 0))


def kernel(
    cfg,
    source,
    receiver,
    classes,
    tables,
    out,
    cheb,
    mirrored,
    cls,
    terms,
    pair_buf,
    ring_buf,
    done_buf,
    load_sem,
    own_cls_sem,
    cls_send,
    cls_recv,
    fwd_send,
    fwd_recv,
    pair_send,
    pair_recv,
    ring_send,
    ring_recv,
    out_send,
    out_recv,
):
    nd, nf, rows_x, cols_y, K, W = (cfg[n] for n in ("nd", "nf", "rows_x", "cols_y", "K", "W"))
    nh = cols_y // LANES
    rows_here = rows_x // nd
    half = rows_here // 2
    groups = nf // 2
    piece = rows_here // nf
    rows_out = rows_x // nf
    owners = nf // nd
    out_parts = rows_out // piece
    wide = (W - rows_here) // 2
    cls_half = W // 2
    scaling = float(nf) ** -0.5

    d = lax.axis_index("depth")
    f = lax.axis_index("freq")
    core = lax.rem(f, 2)
    chip = f // 2
    mate = f + 1 - 2 * core

    def window(depth):
        return pl.multiple_of(jnp.minimum(jnp.maximum(depth * rows_here - wide, 0), rows_x - W), SUB)

    start = window(d)
    base = pl.multiple_of(d * rows_here - start, SUB)

    def remote(src, dst, send, recv, dep, fre):
        return pltpu.make_async_remote_copy(
            src_ref=src,
            dst_ref=dst,
            send_sem=send,
            recv_sem=recv,
            device_id={"depth": dep, "freq": fre},
            device_id_type=pl.DeviceIdType.MESH,
        )

    place = core * half + chip * piece
    goal = d * owners + place // rows_out
    goal_part = lax.rem(place, rows_out) // piece
    from_depth = f // owners

    def giver(part):
        row = lax.rem(f, owners) * rows_out + part * piece
        return 2 * (lax.rem(row, half) // piece) + row // half

    def is_mine(part):
        return jnp.logical_and(from_depth == d, giver(part) == f)

    loads = []
    for comp in range(4):
        ref = source if comp < 2 else receiver
        for h in range(nh):
            loads.append(
                pltpu.make_async_copy(
                    ref.at[0, comp % 2, pl.ds(start, W), pl.ds(h * LANES, LANES)],
                    cheb.at[0, comp, h, pl.ds(SUB, W), :],
                    load_sem.at[comp * nh + h],
                )
            )
            loads[-1].start()
    own_cls = pltpu.make_async_copy(classes.at[0, pl.ds(start, W)], cls.at[d], own_cls_sem)
    own_cls.start()

    barrier = pltpu.get_barrier_semaphore()

    def greet(dep, fre):
        pl.semaphore_signal(
            barrier,
            inc=1,
            device_id={"depth": dep, "freq": fre},
            device_id_type=pl.DeviceIdType.MESH,
        )

    for s in range(1, nd):
        greet(lax.rem(d + s, nd), f)
    greet(d, mate)
    for s in range(1, groups):
        greet(d, 2 * lax.rem(chip + s, groups) + core)
    for part in range(out_parts):

        @pl.when(jnp.logical_not(is_mine(part)))
        def _():
            greet(from_depth, giver(part))

    targets = (nd - 1) + 1 + (groups - 1) + nd
    pl.semaphore_wait(barrier, targets - jnp.where(goal == f, 1, 0))

    cls_rows = pl.multiple_of(core * cls_half, SUB)
    cls_copies = []
    for s in range(1, nd):
        to = lax.rem(d + s, nd)
        src_row = pl.multiple_of(window(to) + cls_rows, SUB)
        copy = remote(
            classes.at[0, pl.ds(src_row, cls_half)],
            cls.at[d, pl.ds(cls_rows, cls_half)],
            cls_send.at[s - 1],
            cls_recv.at[d],
            to,
            f,
        )
        copy.start()
        cls_copies.append(copy)

    def forward(l):
        part = cls.at[l, pl.ds(cls_rows, cls_half)]
        return remote(part, part, fwd_send.at[l], fwd_recv.at[l], d, mate)

    def pass_on(l):
        @pl.when(d != l)
        def _():
            part = cls.at[l, pl.ds(cls_rows, cls_half)]
            remote(part, part, cls_send.at[0], cls_recv.at[l], d, mate).wait_recv()
            forward(l).start()

    def classes_ready(l):
        @pl.when(d != l)
        def _():
            forward(l).wait_recv()

        @pl.when(d == l)
        def _():
            own_cls.wait()

    zero = jnp.zeros((SUB, LANES), jnp.float32)
    for comp in range(4):
        for h in range(nh):
            for k in range(K):
                cheb[k, comp, h, 0:SUB, :] = zero
                cheb[k, comp, h, W + SUB : W + 2 * SUB, :] = zero
            if comp < 2:
                mirrored[comp, h, 0:SUB, :] = zero
                mirrored[comp, h, W + SUB : W + 2 * SUB, :] = zero

    lane = lax.broadcasted_iota(jnp.int32, (SUB, LANES), 1)
    sub = lax.broadcasted_iota(jnp.int32, (SUB, LANES), 0)
    first_lane = lane == 0
    last_lane = lane == LANES - 1

    for copy in loads:
        copy.wait()

    def chebyshev(k):
        def strip(i, carry):
            r0 = pl.multiple_of(i * SUB, SUB)
            for comp in range(4):
                twice, single, along, lefts, rights = [], [], [], [], []
                for h in range(nh):
                    v = cheb[k - 1, comp, h, pl.ds(r0 + SUB, SUB), :]
                    up = cheb[k - 1, comp, h, pl.ds(r0 + SUB - 1, SUB), :]
                    down = cheb[k - 1, comp, h, pl.ds(r0 + SUB + 1, SUB), :]
                    v2 = v + v
                    x_sum = up + down + v2
                    single.append(v)
                    twice.append(v2)
                    along.append(x_sum)
                    lefts.append(pltpu.roll(x_sum, 1, 1))
                    rights.append(pltpu.roll(x_sum, LANES - 1, 1))
                for h in range(nh):
                    left = jnp.where(first_lane, lefts[h - 1] if h > 0 else 0.0, lefts[h])
                    right = jnp.where(last_lane, rights[h + 1] if h + 1 < nh else 0.0, rights[h])
                    total = left + right + (along[h] + along[h])
                    if k == 1:
                        result = 0.125 * total - single[h]
                    else:
                        earlier = cheb[k - 2, comp, h, pl.ds(r0 + SUB, SUB), :]
                        result = 0.25 * total - (twice[h] + earlier)
                    cheb[k, comp, h, pl.ds(r0 + SUB, SUB), :] = result
            return carry

        lax.fori_loop(0, W // SUB, strip, 0)

    def combine(l):
        def strip(i, carry):
            r0 = pl.multiple_of(i * SUB, SUB)
            rows = pl.ds(r0 + SUB, SUB)
            for h in range(nh):
                which = cls[l, pl.ds(r0, SUB), h * LANES : (h + 1) * LANES]
                sums = None
                for k in range(K):
                    cr, ci = (
                        jnp.take_along_axis(
                            jnp.broadcast_to(tables[p * K + k : p * K + k + 1, :], (SUB, LANES)),
                            which,
                            axis=1,
                            mode="promise_in_bounds",
                        )
                        for p in range(2)
                    )
                    sr, si, rr, ri = (cheb[k, comp, h, rows, :] for comp in range(4))
                    new = (
                        cr * sr + ci * si,
                        cr * si - ci * sr,
                        cr * rr - ci * ri,
                        cr * ri + ci * rr,
                    )
                    sums = new if sums is None else tuple(a + b for a, b in zip(sums, new))
                for comp in range(4):
                    cheb[0, comp, h, rows, :] = sums[comp]
                for comp in range(2):
                    mirrored[comp, h, pl.ds(pl.multiple_of(W - r0, SUB), SUB), :] = flip_rows(
                        sums[comp], sub
                    )
            return carry

        lax.fori_loop(0, W // SUB, strip, 0)

    def correlate(l, first):
        def row(i, carry):
            r = first + i
            x = base + r
            for h in range(nh):
                total = None
                for part in range(2):
                    src = mirrored[part, h, pl.ds(W + 3 - x, SUB), :]
                    rec = cheb[0, 2 + part, h, pl.ds(x + 4, SUB), :]
                    total = src * rec if total is None else total + src * rec
                terms[l, r, :, h * LANES : (h + 1) * LANES] = total
            return carry

        lax.fori_loop(0, half, row, 0, unroll=4)

    def pair_copy(l):
        return remote(
            terms.at[l, pl.ds((1 - core) * half, half)],
            pair_buf.at[l],
            pair_send.at[l],
            pair_recv.at[l],
            d,
            mate,
        )

    def ring_copy(l, s):
        other = lax.rem(chip + s, groups)
        return remote(
            terms.at[l, pl.ds(core * half + other * piece, piece)],
            ring_buf.at[l, s - 1],
            ring_send.at[l, s - 1],
            ring_recv.at[l, s - 1],
            d,
            2 * other + core,
        )

    def out_copy(l):
        return remote(
            done_buf.at[l],
            out.at[pl.ds(goal_part * piece, piece), 0],
            out_send.at[l],
            out_recv.at[goal_part],
            l,
            goal,
        )

    def pair_sum(l):
        pair_copy(l).wait_recv()
        for s in list(range(1, groups)) + [0]:
            at = lax.rem(chip + s, groups) * piece
            rows = pl.ds(core * half + at, piece)
            terms[l, rows] = terms[l, rows] + pair_buf[l, pl.ds(at, piece)]
            if s > 0:
                ring_copy(l, s).start()

    def ring_sum(l):
        total = terms[l, pl.ds(place, piece)]
        for s in range(1, groups):
            ring_copy(l, s).wait_recv()
            total = total + ring_buf[l, s - 1]
        total = total * scaling
        mine = jnp.logical_and(l == d, goal == f)

        @pl.when(mine)
        def _():
            out[pl.ds(goal_part * piece, piece), 0] = total

        @pl.when(jnp.logical_not(mine))
        def _():
            done_buf[l] = total
            out_copy(l).start()

    for l in range(nd):
        for k in range(1, K):
            chebyshev(k)
        if l == 0:
            pass_on(0)
        else:
            pair_sum(l - 1)
        classes_ready(l)
        combine(l)
        if l >= 2:
            ring_sum(l - 2)
        correlate(l, (1 - core) * half)
        pair_copy(l).start()
        correlate(l, core * half)
        if l + 1 < nd:
            pass_on(l + 1)
    if nd >= 2:
        ring_sum(nd - 2)
    pair_sum(nd - 1)
    ring_sum(nd - 1)

    for copy in cls_copies:
        copy.wait_send()
    for l in range(nd):

        @pl.when(d != l)
        def _():
            forward(l).wait_send()

        pair_copy(l).wait_send()
        for s in range(1, groups):
            ring_copy(l, s).wait_send()

        @pl.when(jnp.logical_not(jnp.logical_and(l == d, goal == f)))
        def _():
            out_copy(l).wait_send()

    for part in range(out_parts):

        @pl.when(jnp.logical_not(is_mine(part)))
        def _():
            remote(
                done_buf.at[0],
                out.at[pl.ds(part * piece, piece), 0],
                out_send.at[0],
                out_recv.at[part],
                from_depth,
                giver(part),
            ).wait_recv()


def solution(mesh):
    nd, nf = mesh.shape["depth"], mesh.shape["freq"]

    def per_device(source, receiver, classes, coef_table, freq_list):
        rows_x, cols_y = source.shape[2], source.shape[3]
        class_count, K = coef_table.shape[0], coef_table.shape[3]
        rows_here = rows_x // nd
        reach = nd * (K - 1) + H // 2
        wide = -(-reach // SUB) * SUB
        W = min(rows_x, rows_here + 2 * wide)
        nh = cols_y // LANES
        groups = nf // 2
        piece = rows_here // nf
        rows_out = rows_x // nf
        cfg = dict(nd=nd, nf=nf, rows_x=rows_x, cols_y=cols_y, K=K, W=W)
        own = lax.dynamic_index_in_dim(coef_table, freq_list[0], 1, keepdims=False)
        tables = jnp.transpose(own, (1, 2, 0)).reshape(2 * K, class_count)
        tables = jnp.pad(tables, [(0, 0), (0, LANES - class_count)])
        any_space = pl.BlockSpec(memory_space=pl.ANY)
        vmem = pl.BlockSpec(memory_space=pltpu.VMEM)
        dma = pltpu.SemaphoreType.DMA
        return pl.pallas_call(
            functools.partial(kernel, cfg),
            out_shape=jax.ShapeDtypeStruct((rows_out, 1, H, cols_y), jnp.float32),
            in_specs=[any_space, any_space, any_space, vmem],
            out_specs=vmem,
            scratch_shapes=[
                pltpu.VMEM((K, 4, nh, W + 2 * SUB, LANES), jnp.float32),
                pltpu.VMEM((2, nh, W + 2 * SUB, LANES), jnp.float32),
                pltpu.VMEM((nd, W, cols_y), jnp.int32),
                pltpu.VMEM((nd, rows_here, H, cols_y), jnp.float32),
                pltpu.VMEM((nd, rows_here // 2, H, cols_y), jnp.float32),
                pltpu.VMEM((nd, max(groups - 1, 1), piece, H, cols_y), jnp.float32),
                pltpu.VMEM((nd, piece, H, cols_y), jnp.float32),
                dma((4 * nh,)),
                dma,
                dma((nd,)),
                dma((nd,)),
                dma((nd,)),
                dma((nd,)),
                dma((nd,)),
                dma((nd,)),
                dma((nd, max(groups - 1, 1))),
                dma((nd, max(groups - 1, 1))),
                dma((nd,)),
                dma((rows_out // piece,)),
            ],
            compiler_params=pltpu.CompilerParams(
                collective_id=0, has_side_effects=True, vmem_limit_bytes=32 * 1024 * 1024
            ),
        )(source, receiver, classes, tables)

    return jax.shard_map(
        per_device,
        mesh=mesh,
        in_specs=(
            P("freq", None, None, None),
            P("freq", None, None, None),
            P("depth", None, None),
            P(),
            P("freq"),
        ),
        out_specs=P("freq", "depth", None, None),
        check_vma=False,
    )
```

```python
import functools

import jax
import jax.numpy as jnp
from jax import lax
from jax.experimental import pallas as pl
from jax.experimental.pallas import tpu as pltpu
from jax.sharding import PartitionSpec as P

H = 8
LANES = 128
SUB = 8


def flip_rows(v, sub):
    v = pltpu.roll(v, 4, 0)
    v = jnp.where((sub & 2) == 0, pltpu.roll(v, 6, 0), pltpu.roll(v, 2, 0))
    return jnp.where((sub & 1) == 0, pltpu.roll(v, 7, 0), pltpu.roll(v, 1, 0))


def kernel(
    cfg,
    source,
    receiver,
    classes,
    tables,
    out,
    fields,
    other_fields,
    mirrored,
    cls,
    terms,
    pair_buf,
    ring_buf,
    done_buf,
    load_sem,
    own_cls_sem,
    cls_send,
    cls_recv,
    fwd_send,
    fwd_recv,
    pair_send,
    pair_recv,
    ring_send,
    ring_recv,
    out_send,
    out_recv,
    *higher,
):
    nd, nf, rows_x, cols_y, K, W = (cfg[n] for n in ("nd", "nf", "rows_x", "cols_y", "K", "W"))
    nh = cols_y // LANES
    rows_here = rows_x // nd
    half = rows_here // 2
    groups = nf // 2
    piece = rows_here // nf
    rows_out = rows_x // nf
    owners = nf // nd
    out_parts = rows_out // piece
    wide = (W - rows_here) // 2
    cls_half = W // 2
    scaling = float(nf) ** -0.5

    d = lax.axis_index("depth")
    f = lax.axis_index("freq")
    core = lax.rem(f, 2)
    chip = f // 2
    mate = f + 1 - 2 * core

    def window(depth):
        return pl.multiple_of(jnp.minimum(jnp.maximum(depth * rows_here - wide, 0), rows_x - W), SUB)

    start = window(d)
    base = pl.multiple_of(d * rows_here - start, SUB)

    def remote(src, dst, send, recv, dep, fre):
        return pltpu.make_async_remote_copy(
            src_ref=src,
            dst_ref=dst,
            send_sem=send,
            recv_sem=recv,
            device_id={"depth": dep, "freq": fre},
            device_id_type=pl.DeviceIdType.MESH,
        )

    place = core * half + chip * piece
    goal = d * owners + place // rows_out
    goal_part = lax.rem(place, rows_out) // piece
    from_depth = f // owners

    def giver(part):
        row = lax.rem(f, owners) * rows_out + part * piece
        return 2 * (lax.rem(row, half) // piece) + row // half

    def is_mine(part):
        return jnp.logical_and(from_depth == d, giver(part) == f)

    loads = []
    for comp in range(4):
        ref = source if comp < 2 else receiver
        for h in range(nh):
            loads.append(
                pltpu.make_async_copy(
                    ref.at[0, comp % 2, pl.ds(start, W), pl.ds(h * LANES, LANES)],
                    fields.at[comp, h, pl.ds(SUB, W), :],
                    load_sem.at[comp * nh + h],
                )
            )
            loads[-1].start()
    own_cls = pltpu.make_async_copy(classes.at[0, pl.ds(start, W)], cls.at[d], own_cls_sem)
    own_cls.start()

    barrier = pltpu.get_barrier_semaphore()

    def greet(dep, fre):
        pl.semaphore_signal(
            barrier,
            inc=1,
            device_id={"depth": dep, "freq": fre},
            device_id_type=pl.DeviceIdType.MESH,
        )

    for s in range(1, nd):
        greet(lax.rem(d + s, nd), f)
    greet(d, mate)
    for s in range(1, groups):
        greet(d, 2 * lax.rem(chip + s, groups) + core)
    for part in range(out_parts):

        @pl.when(jnp.logical_not(is_mine(part)))
        def _():
            greet(from_depth, giver(part))

    targets = (nd - 1) + 1 + (groups - 1) + nd
    pl.semaphore_wait(barrier, targets - jnp.where(goal == f, 1, 0))

    cls_rows = pl.multiple_of(core * cls_half, SUB)
    cls_copies = []
    for s in range(1, nd):
        to = lax.rem(d + s, nd)
        src_row = pl.multiple_of(window(to) + cls_rows, SUB)
        copy = remote(
            classes.at[0, pl.ds(src_row, cls_half)],
            cls.at[d, pl.ds(cls_rows, cls_half)],
            cls_send.at[s - 1],
            cls_recv.at[d],
            to,
            f,
        )
        copy.start()
        cls_copies.append(copy)

    def forward(l):
        part = cls.at[l, pl.ds(cls_rows, cls_half)]
        return remote(part, part, fwd_send.at[l], fwd_recv.at[l], d, mate)

    def pass_on(l):
        @pl.when(d != l)
        def _():
            part = cls.at[l, pl.ds(cls_rows, cls_half)]
            remote(part, part, cls_send.at[0], cls_recv.at[l], d, mate).wait_recv()
            forward(l).start()

    def classes_ready(l):
        @pl.when(d != l)
        def _():
            forward(l).wait_recv()

        @pl.when(d == l)
        def _():
            own_cls.wait()

    zero = jnp.zeros((SUB, LANES), jnp.float32)
    for comp in range(4):
        for h in range(nh):
            for ref in (fields, other_fields) + higher:
                ref[comp, h, 0:SUB, :] = zero
                ref[comp, h, W + SUB : W + 2 * SUB, :] = zero
            if comp < 2:
                mirrored[comp, h, 0:SUB, :] = zero
                mirrored[comp, h, W + SUB : W + 2 * SUB, :] = zero

    lane = lax.broadcasted_iota(jnp.int32, (SUB, LANES), 1)
    sub = lax.broadcasted_iota(jnp.int32, (SUB, LANES), 0)
    first_lane = lane == 0
    last_lane = lane == LANES - 1

    for copy in loads:
        copy.wait()

    def reach_of(l, extra):
        margin = (nd - 1 - l) * (K - 1) + H // 2 + extra
        margin = -(-margin // SUB) * SUB
        rows = min(W, rows_here + 2 * margin)
        begin = jnp.minimum(jnp.maximum(base - margin, 0), W - rows)
        return begin, rows // SUB

    def strips(l, extra, group, body):
        begin, count = reach_of(l, extra)
        group = next(g for g in range(min(group, count), 0, -1) if count % g == 0)

        def step(i, carry):
            for g in range(group):
                body(pl.multiple_of(begin + i * (group * SUB) + g * SUB, SUB))
            return carry

        lax.fori_loop(0, count // group, step, 0)

    def chebyshev(l, k):
        held = (fields if l % 2 == 0 else other_fields,) + higher

        def strip(r0):
            for comp in range(4):
                twice, single, along, lefts, rights = [], [], [], [], []
                for h in range(nh):
                    v = held[k - 1][comp, h, pl.ds(r0 + SUB, SUB), :]
                    up = held[k - 1][comp, h, pl.ds(r0 + SUB - 1, SUB), :]
                    down = held[k - 1][comp, h, pl.ds(r0 + SUB + 1, SUB), :]
                    v2 = v + v
                    x_sum = up + down + v2
                    single.append(v)
                    twice.append(v2)
                    along.append(x_sum)
                    lefts.append(pltpu.roll(x_sum, 1, 1))
                    rights.append(pltpu.roll(x_sum, LANES - 1, 1))
                for h in range(nh):
                    left = jnp.where(first_lane, lefts[h - 1] if h > 0 else 0.0, lefts[h])
                    right = jnp.where(last_lane, rights[h + 1] if h + 1 < nh else 0.0, rights[h])
                    total = left + right + (along[h] + along[h])
                    if k == 1:
                        result = 0.125 * total - single[h]
                    else:
                        earlier = held[k - 2][comp, h, pl.ds(r0 + SUB, SUB), :]
                        result = 0.25 * total - (twice[h] + earlier)
                    held[k][comp, h, pl.ds(r0 + SUB, SUB), :] = result

        strips(l, K - 2, 7, strip)

    def combine(l):
        held = (fields if l % 2 == 0 else other_fields,) + higher
        result = other_fields if l % 2 == 0 else fields

        def strip(r0):
            rows = pl.ds(r0 + SUB, SUB)
            for h in range(nh):
                which = cls[l, pl.ds(r0, SUB), h * LANES : (h + 1) * LANES]
                sums = None
                for k in range(K):
                    cr, ci = (
                        jnp.take_along_axis(
                            jnp.broadcast_to(tables[p * K + k : p * K + k + 1, :], (SUB, LANES)),
                            which,
                            axis=1,
                            mode="promise_in_bounds",
                        )
                        for p in range(2)
                    )
                    sr, si, rr, ri = (held[k][comp, h, rows, :] for comp in range(4))
                    new = (
                        cr * sr + ci * si,
                        cr * si - ci * sr,
                        cr * rr - ci * ri,
                        cr * ri + ci * rr,
                    )
                    sums = new if sums is None else tuple(a + b for a, b in zip(sums, new))
                for comp in range(4):
                    result[comp, h, rows, :] = sums[comp]
                for comp in range(2):
                    mirrored[comp, h, pl.ds(pl.multiple_of(W - r0, SUB), SUB), :] = flip_rows(
                        sums[comp], sub
                    )

        strips(l, 0, 2, strip)

    def correlate(l, first):
        result = other_fields if l % 2 == 0 else fields
        group = min(8, half)

        def step(i, carry):
            for g in range(group):
                r = first + i * group + g
                x = base + r
                for h in range(nh):
                    total = None
                    for part in range(2):
                        src = mirrored[part, h, pl.ds(W + 3 - x, SUB), :]
                        rec = result[2 + part, h, pl.ds(x + 4, SUB), :]
                        total = src * rec if total is None else total + src * rec
                    terms[l, r, :, h * LANES : (h + 1) * LANES] = total
            return carry

        lax.fori_loop(0, half // group, step, 0)

    def pair_copy(l):
        return remote(
            terms.at[l, pl.ds((1 - core) * half, half)],
            pair_buf.at[l],
            pair_send.at[l],
            pair_recv.at[l],
            d,
            mate,
        )

    def ring_copy(l, s):
        other = lax.rem(chip + s, groups)
        return remote(
            terms.at[l, pl.ds(core * half + other * piece, piece)],
            ring_buf.at[l, s - 1],
            ring_send.at[l, s - 1],
            ring_recv.at[l, s - 1],
            d,
            2 * other + core,
        )

    def out_copy(l):
        return remote(
            done_buf.at[l],
            out.at[pl.ds(goal_part * piece, piece), 0],
            out_send.at[l],
            out_recv.at[goal_part],
            l,
            goal,
        )

    def pair_sum(l):
        pair_copy(l).wait_recv()
        for s in list(range(1, groups)) + [0]:
            at = lax.rem(chip + s, groups) * piece
            rows = pl.ds(core * half + at, piece)
            terms[l, rows] = terms[l, rows] + pair_buf[l, pl.ds(at, piece)]
            if s > 0:
                ring_copy(l, s).start()

    def ring_sum(l):
        total = terms[l, pl.ds(place, piece)]
        for s in range(1, groups):
            ring_copy(l, s).wait_recv()
            total = total + ring_buf[l, s - 1]
        total = total * scaling
        mine = jnp.logical_and(l == d, goal == f)

        @pl.when(mine)
        def _():
            out[pl.ds(goal_part * piece, piece), 0] = total

        @pl.when(jnp.logical_not(mine))
        def _():
            done_buf[l] = total
            out_copy(l).start()

    for l in range(nd):
        for k in range(1, K):
            chebyshev(l, k)
        if l == 0:
            pass_on(0)
        else:
            pair_sum(l - 1)
        classes_ready(l)
        combine(l)
        if l >= 2:
            ring_sum(l - 2)
        correlate(l, (1 - core) * half)
        pair_copy(l).start()
        correlate(l, core * half)
        if l + 1 < nd:
            pass_on(l + 1)
    if nd >= 2:
        ring_sum(nd - 2)
    pair_sum(nd - 1)
    ring_sum(nd - 1)

    for copy in cls_copies:
        copy.wait_send()
    for l in range(nd):

        @pl.when(d != l)
        def _():
            forward(l).wait_send()

        pair_copy(l).wait_send()
        for s in range(1, groups):
            ring_copy(l, s).wait_send()

        @pl.when(jnp.logical_not(jnp.logical_and(l == d, goal == f)))
        def _():
            out_copy(l).wait_send()

    for part in range(out_parts):

        @pl.when(jnp.logical_not(is_mine(part)))
        def _():
            remote(
                done_buf.at[0],
                out.at[pl.ds(part * piece, piece), 0],
                out_send.at[0],
                out_recv.at[part],
                from_depth,
                giver(part),
            ).wait_recv()


def solution(mesh):
    nd, nf = mesh.shape["depth"], mesh.shape["freq"]

    def per_device(source, receiver, classes, coef_table, freq_list):
        rows_x, cols_y = source.shape[2], source.shape[3]
        class_count, K = coef_table.shape[0], coef_table.shape[3]
        rows_here = rows_x // nd
        reach = nd * (K - 1) + H // 2
        wide = -(-reach // SUB) * SUB
        W = min(rows_x, rows_here + 2 * wide)
        nh = cols_y // LANES
        groups = nf // 2
        piece = rows_here // nf
        rows_out = rows_x // nf
        cfg = dict(nd=nd, nf=nf, rows_x=rows_x, cols_y=cols_y, K=K, W=W)
        own = lax.dynamic_index_in_dim(coef_table, freq_list[0], 1, keepdims=False)
        tables = jnp.transpose(own, (1, 2, 0)).reshape(2 * K, class_count)
        tables = jnp.pad(tables, [(0, 0), (0, LANES - class_count)])
        hbm = pl.BlockSpec(memory_space=pltpu.HBM)
        vmem = pl.BlockSpec(memory_space=pltpu.VMEM)
        dma = pltpu.SemaphoreType.DMA
        field = pltpu.VMEM((4, nh, W + 2 * SUB, LANES), jnp.float32)
        return pl.pallas_call(
            functools.partial(kernel, cfg),
            out_shape=jax.ShapeDtypeStruct((rows_out, 1, H, cols_y), jnp.float32),
            in_specs=[hbm, hbm, hbm, vmem],
            out_specs=vmem,
            scratch_shapes=[
                field,
                field,
                pltpu.VMEM((2, nh, W + 2 * SUB, LANES), jnp.float32),
                pltpu.VMEM((nd, W, cols_y), jnp.int32),
                pltpu.VMEM((nd, rows_here, H, cols_y), jnp.float32),
                pltpu.VMEM((nd, rows_here // 2, H, cols_y), jnp.float32),
                pltpu.VMEM((nd, max(groups - 1, 1), piece, H, cols_y), jnp.float32),
                pltpu.VMEM((nd, piece, H, cols_y), jnp.float32),
                dma((4 * nh,)),
                dma,
                dma((nd,)),
                dma((nd,)),
                dma((nd,)),
                dma((nd,)),
                dma((nd,)),
                dma((nd,)),
                dma((nd, max(groups - 1, 1))),
                dma((nd, max(groups - 1, 1))),
                dma((nd,)),
                dma((rows_out // piece,)),
            ]
            + [field] * (K - 1),
            compiler_params=pltpu.CompilerParams(
                collective_id=0, has_side_effects=True, vmem_limit_bytes=62 * 1024 * 1024
            ),
        )(source, receiver, classes, tables)

    return jax.shard_map(
        per_device,
        mesh=mesh,
        in_specs=(
            P("freq", None, None, None),
            P("freq", None, None, None),
            P("depth", None, None),
            P(),
            P("freq"),
        ),
        out_specs=P("freq", "depth", None, None),
        check_vma=False,
    )
```

```python
import functools

import jax
import jax.numpy as jnp
from jax import lax
from jax.experimental import pallas as pl
from jax.experimental.pallas import tpu as pltpu
from jax.sharding import PartitionSpec as P

H = 8
LANES = 128
SUB = 8


def flip_rows(v, sub):
    v = pltpu.roll(v, 4, 0)
    v = jnp.where((sub & 2) == 0, pltpu.roll(v, 6, 0), pltpu.roll(v, 2, 0))
    return jnp.where((sub & 1) == 0, pltpu.roll(v, 7, 0), pltpu.roll(v, 1, 0))


def kernel(
    cfg,
    source,
    receiver,
    classes,
    coef,
    freq_row,
    out,
    tables,
    fields,
    mirrored,
    cls,
    terms,
    pair_buf,
    ring_buf,
    done_buf,
    load_sem,
    own_cls_sem,
    cls_send,
    cls_recv,
    fwd_send,
    fwd_recv,
    pair_send,
    pair_recv,
    ring_send,
    ring_recv,
    out_send,
    out_recv,
    *higher,
):
    nd, nf, rows_x, cols_y, K, W = (cfg[n] for n in ("nd", "nf", "rows_x", "cols_y", "K", "W"))
    nh = cols_y // LANES
    rows_here = rows_x // nd
    half = rows_here // 2
    groups = nf // 2
    piece = rows_here // nf
    rows_out = rows_x // nf
    owners = nf // nd
    out_parts = rows_out // piece
    wide = (W - rows_here) // 2
    cls_half = W // 2

    d = lax.axis_index("depth")
    f = lax.axis_index("freq")
    core = lax.rem(f, 2)
    chip = f // 2
    mate = f + 1 - 2 * core

    def window(depth):
        return pl.multiple_of(jnp.minimum(jnp.maximum(depth * rows_here - wide, 0), rows_x - W), SUB)

    start = window(d)
    base = pl.multiple_of(d * rows_here - start, SUB)

    def remote(src, dst, send, recv, dep, fre):
        return pltpu.make_async_remote_copy(
            src_ref=src,
            dst_ref=dst,
            send_sem=send,
            recv_sem=recv,
            device_id={"depth": dep, "freq": fre},
            device_id_type=pl.DeviceIdType.MESH,
        )

    place = core * half + chip * piece
    goal = d * owners + place // rows_out
    goal_part = lax.rem(place, rows_out) // piece
    from_depth = f // owners

    def giver(part):
        row = lax.rem(f, owners) * rows_out + part * piece
        return 2 * (lax.rem(row, half) // piece) + row // half

    def is_mine(part):
        return jnp.logical_and(from_depth == d, giver(part) == f)

    loads = []
    for comp in range(4):
        ref = source if comp < 2 else receiver
        for h in range(nh):
            loads.append(
                pltpu.make_async_copy(
                    ref.at[0, comp % 2, pl.ds(start, W), pl.ds(h * LANES, LANES)],
                    fields.at[comp, h, pl.ds(SUB, W), :],
                    load_sem.at[comp * nh + h],
                )
            )
            loads[-1].start()
    own_cls = pltpu.make_async_copy(classes.at[0, pl.ds(start, W)], cls.at[d], own_cls_sem)
    own_cls.start()

    barrier = pltpu.get_barrier_semaphore()

    def greet(dep, fre):
        pl.semaphore_signal(
            barrier,
            inc=1,
            device_id={"depth": dep, "freq": fre},
            device_id_type=pl.DeviceIdType.MESH,
        )

    for s in range(1, nd):
        greet(lax.rem(d + s, nd), f)
    greet(d, mate)
    for s in range(1, groups):
        greet(d, 2 * lax.rem(chip + s, groups) + core)
    for part in range(out_parts):

        @pl.when(jnp.logical_not(is_mine(part)))
        def _():
            greet(from_depth, giver(part))

    targets = (nd - 1) + 1 + (groups - 1) + nd
    pl.semaphore_wait(barrier, targets - jnp.where(goal == f, 1, 0))

    cls_rows = pl.multiple_of(core * cls_half, SUB)
    cls_copies = []
    for s in range(1, nd):
        to = lax.rem(d + s, nd)
        src_row = pl.multiple_of(window(to) + cls_rows, SUB)
        copy = remote(
            classes.at[0, pl.ds(src_row, cls_half)],
            cls.at[d, pl.ds(cls_rows, cls_half)],
            cls_send.at[s - 1],
            cls_recv.at[d],
            to,
            f,
        )
        copy.start()
        cls_copies.append(copy)

    def forward(l):
        part = cls.at[l, pl.ds(cls_rows, cls_half)]
        return remote(part, part, fwd_send.at[l], fwd_recv.at[l], d, mate)

    def pass_on(l):
        @pl.when(d != l)
        def _():
            part = cls.at[l, pl.ds(cls_rows, cls_half)]
            remote(part, part, cls_send.at[0], cls_recv.at[l], d, mate).wait_recv()
            forward(l).start()

    def classes_ready(l):
        @pl.when(d != l)
        def _():
            forward(l).wait_recv()

        @pl.when(d == l)
        def _():
            own_cls.wait()

    held = (fields,) + higher
    row = freq_row[0]
    for k in range(K):
        for p in range(2):
            at = p * K + k
            tables[at : at + 1, 0 : coef.shape[3]] = coef[row, k, p : p + 1, :]
    zero = jnp.zeros((SUB, LANES), jnp.float32)
    for comp in range(4):
        for h in range(nh):
            for ref in held:
                ref[comp, h, 0:SUB, :] = zero
                ref[comp, h, W + SUB : W + 2 * SUB, :] = zero
            if comp < 2:
                mirrored[comp, h, 0:SUB, :] = zero
                mirrored[comp, h, W + SUB : W + 2 * SUB, :] = zero

    lane = lax.broadcasted_iota(jnp.int32, (SUB, LANES), 1)
    sub = lax.broadcasted_iota(jnp.int32, (SUB, LANES), 0)
    first_lane = lane == 0
    last_lane = lane == LANES - 1

    for copy in loads:
        copy.wait()

    def chebyshev(k):
        for r0 in range(0, W, SUB):
            for comp in range(4):
                twice, single, along, lefts, rights = [], [], [], [], []
                for h in range(nh):
                    v = held[k - 1][comp, h, pl.ds(r0 + SUB, SUB), :]
                    up = held[k - 1][comp, h, pl.ds(r0 + SUB - 1, SUB), :]
                    down = held[k - 1][comp, h, pl.ds(r0 + SUB + 1, SUB), :]
                    v2 = v + v
                    x_sum = up + down + v2
                    single.append(v)
                    twice.append(v2)
                    along.append(x_sum)
                    lefts.append(pltpu.roll(x_sum, 1, 1))
                    rights.append(pltpu.roll(x_sum, LANES - 1, 1))
                for h in range(nh):
                    left = jnp.where(first_lane, lefts[h - 1] if h > 0 else 0.0, lefts[h])
                    right = jnp.where(last_lane, rights[h + 1] if h + 1 < nh else 0.0, rights[h])
                    total = left + right + (along[h] + along[h])
                    if k == 1:
                        result = 0.125 * total - single[h]
                    else:
                        earlier = held[k - 2][comp, h, pl.ds(r0 + SUB, SUB), :]
                        result = 0.25 * total - (twice[h] + earlier)
                    held[k][comp, h, pl.ds(r0 + SUB, SUB), :] = result

    def combine(l):
        for r0 in range(0, W, SUB):
            rows = pl.ds(r0 + SUB, SUB)
            for h in range(nh):
                which = cls[l, pl.ds(r0, SUB), h * LANES : (h + 1) * LANES]
                sums = None
                for k in range(K):
                    cr, ci = (
                        jnp.take_along_axis(
                            jnp.broadcast_to(tables[p * K + k : p * K + k + 1, :], (SUB, LANES)),
                            which,
                            axis=1,
                            mode="promise_in_bounds",
                        )
                        for p in range(2)
                    )
                    sr, si, rr, ri = (held[k][comp, h, rows, :] for comp in range(4))
                    new = (
                        cr * sr + ci * si,
                        cr * si - ci * sr,
                        cr * rr - ci * ri,
                        cr * ri + ci * rr,
                    )
                    sums = new if sums is None else tuple(a + b for a, b in zip(sums, new))
                for comp in range(4):
                    fields[comp, h, rows, :] = sums[comp]
                for comp in range(2):
                    mirrored[comp, h, pl.ds(W - r0, SUB), :] = flip_rows(
                        sums[comp], sub
                    )

    def correlate(l, first):
        group = min(16, half)

        def step(i, carry):
            for g in range(group):
                r = first + i * group + g
                x = base + r
                for h in range(nh):
                    total = None
                    for part in range(2):
                        src = mirrored[part, h, pl.ds(W + 3 - x, SUB), :]
                        rec = fields[2 + part, h, pl.ds(x + 4, SUB), :]
                        total = src * rec if total is None else total + src * rec
                    terms[l, r, :, h * LANES : (h + 1) * LANES] = total
            return carry

        lax.fori_loop(0, half // group, step, 0)

    def pair_copy(l):
        return remote(
            terms.at[l, pl.ds((1 - core) * half, half)],
            pair_buf.at[l],
            pair_send.at[l],
            pair_recv.at[l],
            d,
            mate,
        )

    def ring_copy(l, s):
        other = lax.rem(chip + s, groups)
        return remote(
            terms.at[l, pl.ds(core * half + other * piece, piece)],
            ring_buf.at[l, s - 1],
            ring_send.at[l, s - 1],
            ring_recv.at[l, s - 1],
            d,
            2 * other + core,
        )

    def out_copy(l):
        return remote(
            done_buf.at[l],
            out.at[pl.ds(goal_part * piece, piece), 0],
            out_send.at[l],
            out_recv.at[goal_part],
            l,
            goal,
        )

    def pair_sum(l):
        pair_copy(l).wait_recv()
        for s in list(range(1, groups)) + [0]:
            at = lax.rem(chip + s, groups) * piece
            rows = pl.ds(core * half + at, piece)
            terms[l, rows] = terms[l, rows] + pair_buf[l, pl.ds(at, piece)]
            if s > 0:
                ring_copy(l, s).start()

    def ring_sum(l):
        total = terms[l, pl.ds(place, piece)]
        for s in range(1, groups):
            ring_copy(l, s).wait_recv()
            total = total + ring_buf[l, s - 1]
        mine = jnp.logical_and(l == d, goal == f)

        @pl.when(mine)
        def _():
            out[pl.ds(goal_part * piece, piece), 0] = total

        @pl.when(jnp.logical_not(mine))
        def _():
            done_buf[l] = total
            out_copy(l).start()

    def level(l, carry):
        for k in range(1, K):
            chebyshev(k)

        @pl.when(l == 0)
        def _():
            pass_on(0)

        @pl.when(l > 0)
        def _():
            pair_sum(l - 1)

        classes_ready(l)
        combine(l)
        correlate(l, (1 - core) * half)
        pair_copy(l).start()
        correlate(l, core * half)

        @pl.when(l + 1 < nd)
        def _():
            pass_on(l + 1)

        @pl.when(l > 1)
        def _():
            ring_sum(l - 2)

        return carry

    lax.fori_loop(0, nd, level, 0)
    if nd >= 2:
        ring_sum(nd - 2)
    pair_sum(nd - 1)
    ring_sum(nd - 1)

    for copy in cls_copies:
        copy.wait_send()
    for l in range(nd):

        @pl.when(d != l)
        def _():
            forward(l).wait_send()

        pair_copy(l).wait_send()
        for s in range(1, groups):
            ring_copy(l, s).wait_send()

        @pl.when(jnp.logical_not(jnp.logical_and(l == d, goal == f)))
        def _():
            out_copy(l).wait_send()

    for part in range(out_parts):

        @pl.when(jnp.logical_not(is_mine(part)))
        def _():
            remote(
                done_buf.at[0],
                out.at[pl.ds(part * piece, piece), 0],
                out_send.at[0],
                out_recv.at[part],
                from_depth,
                giver(part),
            ).wait_recv()


def solution(mesh):
    nd, nf = mesh.shape["depth"], mesh.shape["freq"]

    def per_device(source, receiver, classes, coef_table, freq_list):
        rows_x, cols_y = source.shape[2], source.shape[3]
        K = coef_table.shape[3]
        rows_here = rows_x // nd
        reach = nd * (K - 1) + H // 2
        wide = -(-reach // SUB) * SUB
        W = min(rows_x, rows_here + 2 * wide)
        nh = cols_y // LANES
        groups = nf // 2
        piece = rows_here // nf
        rows_out = rows_x // nf
        cfg = dict(nd=nd, nf=nf, rows_x=rows_x, cols_y=cols_y, K=K, W=W)
        coef = jnp.transpose(coef_table, (1, 3, 2, 0))
        hbm = pl.BlockSpec(memory_space=pltpu.HBM)
        vmem = pl.BlockSpec(memory_space=pltpu.VMEM)
        dma = pltpu.SemaphoreType.DMA
        field = pltpu.VMEM((4, nh, W + 2 * SUB, LANES), jnp.float32)
        summed = pl.pallas_call(
            functools.partial(kernel, cfg),
            out_shape=jax.ShapeDtypeStruct((rows_out, 1, H, cols_y), jnp.float32),
            in_specs=[hbm, hbm, hbm, vmem, pl.BlockSpec(memory_space=pltpu.SMEM)],
            out_specs=vmem,
            scratch_shapes=[
                pltpu.VMEM((2 * K, LANES), jnp.float32),
                field,
                pltpu.VMEM((2, nh, W + 2 * SUB, LANES), jnp.float32),
                pltpu.VMEM((nd, W, cols_y), jnp.int32),
                pltpu.VMEM((nd, rows_here, H, cols_y), jnp.float32),
                pltpu.VMEM((nd, rows_here // 2, H, cols_y), jnp.float32),
                pltpu.VMEM((nd, max(groups - 1, 1), piece, H, cols_y), jnp.float32),
                pltpu.VMEM((nd, piece, H, cols_y), jnp.float32),
                dma((4 * nh,)),
                dma,
                dma((nd,)),
                dma((nd,)),
                dma((nd,)),
                dma((nd,)),
                dma((nd,)),
                dma((nd,)),
                dma((nd, max(groups - 1, 1))),
                dma((nd, max(groups - 1, 1))),
                dma((nd,)),
                dma((rows_out // piece,)),
            ]
            + [field] * (K - 1),
            compiler_params=pltpu.CompilerParams(
                collective_id=0, has_side_effects=True, vmem_limit_bytes=62 * 1024 * 1024
            ),
        )(source, receiver, classes, coef, freq_list)
        return summed * float(nf) ** -0.5

    return jax.shard_map(
        per_device,
        mesh=mesh,
        in_specs=(
            P("freq", None, None, None),
            P("freq", None, None, None),
            P("depth", None, None),
            P(),
            P("freq"),
        ),
        out_specs=P("freq", "depth", None, None),
        check_vma=False,
    )
```

```python
import functools

import jax
import jax.numpy as jnp
from jax import lax
from jax.experimental import pallas as pl
from jax.experimental.pallas import tpu as pltpu
from jax.sharding import PartitionSpec as P

H = 8
LANES = 128
SUB = 8


def flip_rows(v, sub):
    v = pltpu.roll(v, 4, 0)
    v = jnp.where((sub & 2) == 0, pltpu.roll(v, 6, 0), pltpu.roll(v, 2, 0))
    return jnp.where((sub & 1) == 0, pltpu.roll(v, 7, 0), pltpu.roll(v, 1, 0))


def kernel(
    cfg,
    source,
    receiver,
    classes,
    coef,
    freq_row,
    out,
    tables,
    fields,
    mirrored,
    cls,
    terms,
    pair_buf,
    ring_buf,
    done_buf,
    load_sem,
    own_cls_sem,
    cls_send,
    cls_recv,
    fwd_send,
    fwd_recv,
    pair_send,
    pair_recv,
    ring_send,
    ring_recv,
    out_send,
    out_recv,
    *higher,
):
    nd, nf, rows_x, cols_y, K, W = (cfg[n] for n in ("nd", "nf", "rows_x", "cols_y", "K", "W"))
    nh = cols_y // LANES
    rows_here = rows_x // nd
    half = rows_here // 2
    groups = nf // 2
    piece = rows_here // nf
    rows_out = rows_x // nf
    owners = nf // nd
    out_parts = rows_out // piece
    wide = (W - rows_here) // 2
    cls_half = W // 2

    d = lax.axis_index("depth")
    f = lax.axis_index("freq")
    core = lax.rem(f, 2)
    chip = f // 2
    mate = f + 1 - 2 * core

    def window(depth):
        return pl.multiple_of(jnp.minimum(jnp.maximum(depth * rows_here - wide, 0), rows_x - W), SUB)

    start = window(d)
    base = pl.multiple_of(d * rows_here - start, SUB)

    def remote(src, dst, send, recv, dep, fre):
        return pltpu.make_async_remote_copy(
            src_ref=src,
            dst_ref=dst,
            send_sem=send,
            recv_sem=recv,
            device_id={"depth": dep, "freq": fre},
            device_id_type=pl.DeviceIdType.MESH,
        )

    place = core * half + chip * piece
    goal = d * owners + place // rows_out
    goal_part = lax.rem(place, rows_out) // piece
    from_depth = f // owners

    def giver(part):
        row = lax.rem(f, owners) * rows_out + part * piece
        return 2 * (lax.rem(row, half) // piece) + row // half

    def is_mine(part):
        return jnp.logical_and(from_depth == d, giver(part) == f)

    loads = []
    for comp in range(4):
        ref = source if comp < 2 else receiver
        for h in range(nh):
            loads.append(
                pltpu.make_async_copy(
                    ref.at[0, comp % 2, pl.ds(start, W), pl.ds(h * LANES, LANES)],
                    fields.at[comp, h, pl.ds(SUB, W), :],
                    load_sem.at[comp * nh + h],
                )
            )
            loads[-1].start()
    own_cls = pltpu.make_async_copy(classes.at[0, pl.ds(start, W)], cls.at[d], own_cls_sem)
    own_cls.start()

    barrier = pltpu.get_barrier_semaphore()

    def greet(dep, fre):
        pl.semaphore_signal(
            barrier,
            inc=1,
            device_id={"depth": dep, "freq": fre},
            device_id_type=pl.DeviceIdType.MESH,
        )

    for s in range(1, nd):
        greet(lax.rem(d + s, nd), f)
    greet(d, mate)
    for s in range(1, groups):
        greet(d, 2 * lax.rem(chip + s, groups) + core)
    for part in range(out_parts):

        @pl.when(jnp.logical_not(is_mine(part)))
        def _():
            greet(from_depth, giver(part))

    targets = (nd - 1) + 1 + (groups - 1) + nd
    pl.semaphore_wait(barrier, targets - jnp.where(goal == f, 1, 0))

    cls_rows = pl.multiple_of(core * cls_half, SUB)
    cls_copies = []
    for s in range(nd - 1, 0, -1):
        to = lax.rem(d + s, nd)
        src_row = pl.multiple_of(window(to) + cls_rows, SUB)
        copy = remote(
            classes.at[0, pl.ds(src_row, cls_half)],
            cls.at[d, pl.ds(cls_rows, cls_half)],
            cls_send.at[s - 1],
            cls_recv.at[d],
            to,
            f,
        )
        cls_copies.append(copy)

    @pl.when(d == 0)
    def _():
        for copy in cls_copies:
            copy.start()


    def forward(l):
        part = cls.at[l, pl.ds(cls_rows, cls_half)]
        return remote(part, part, fwd_send.at[l], fwd_recv.at[l], d, mate)

    def pass_on(l):
        @pl.when(d != l)
        def _():
            part = cls.at[l, pl.ds(cls_rows, cls_half)]
            remote(part, part, cls_send.at[0], cls_recv.at[l], d, mate).wait_recv()
            forward(l).start()

    def classes_ready(l):
        @pl.when(d != l)
        def _():
            forward(l).wait_recv()

        @pl.when(d == l)
        def _():
            own_cls.wait()

    held = (fields,) + higher
    row = freq_row[0]
    for k in range(K):
        for p in range(2):
            at = p * K + k
            tables[at : at + 1, 0 : coef.shape[3]] = coef[row, k, p : p + 1, :]
    zero = jnp.zeros((SUB, LANES), jnp.float32)
    for comp in range(4):
        for h in range(nh):
            for ref in held:
                ref[comp, h, 0:SUB, :] = zero
                ref[comp, h, W + SUB : W + 2 * SUB, :] = zero
            if comp < 2:
                mirrored[comp, h, 0:SUB, :] = zero
                mirrored[comp, h, W + SUB : W + 2 * SUB, :] = zero

    lane = lax.broadcasted_iota(jnp.int32, (SUB, LANES), 1)
    sub = lax.broadcasted_iota(jnp.int32, (SUB, LANES), 0)
    first_lane = lane == 0
    last_lane = lane == LANES - 1

    for copy in loads:
        copy.wait()

    def chebyshev(k):
        for r0 in range(0, W, SUB):
            for comp in range(4):
                twice, single, along, lefts, rights = [], [], [], [], []
                for h in range(nh):
                    v = held[k - 1][comp, h, pl.ds(r0 + SUB, SUB), :]
                    up = held[k - 1][comp, h, pl.ds(r0 + SUB - 1, SUB), :]
                    down = held[k - 1][comp, h, pl.ds(r0 + SUB + 1, SUB), :]
                    v2 = v + v
                    x_sum = up + down + v2
                    single.append(v)
                    twice.append(v2)
                    along.append(x_sum)
                    lefts.append(pltpu.roll(x_sum, 1, 1))
                    rights.append(pltpu.roll(x_sum, LANES - 1, 1))
                for h in range(nh):
                    left = jnp.where(first_lane, lefts[h - 1] if h > 0 else 0.0, lefts[h])
                    right = jnp.where(last_lane, rights[h + 1] if h + 1 < nh else 0.0, rights[h])
                    total = left + right + (along[h] + along[h])
                    if k == 1:
                        result = 0.125 * total - single[h]
                    else:
                        earlier = held[k - 2][comp, h, pl.ds(r0 + SUB, SUB), :]
                        result = 0.25 * total - (twice[h] + earlier)
                    held[k][comp, h, pl.ds(r0 + SUB, SUB), :] = result

    def combine(l):
        for r0 in range(0, W, SUB):
            rows = pl.ds(r0 + SUB, SUB)
            for h in range(nh):
                which = cls[l, pl.ds(r0, SUB), h * LANES : (h + 1) * LANES]
                sums = None
                for k in range(K):
                    cr, ci = (
                        jnp.take_along_axis(
                            jnp.broadcast_to(tables[p * K + k : p * K + k + 1, :], (SUB, LANES)),
                            which,
                            axis=1,
                            mode="promise_in_bounds",
                        )
                        for p in range(2)
                    )
                    sr, si, rr, ri = (held[k][comp, h, rows, :] for comp in range(4))
                    new = (
                        cr * sr + ci * si,
                        cr * si - ci * sr,
                        cr * rr - ci * ri,
                        cr * ri + ci * rr,
                    )
                    sums = new if sums is None else tuple(a + b for a, b in zip(sums, new))
                for comp in range(4):
                    fields[comp, h, rows, :] = sums[comp]
                for comp in range(2):
                    mirrored[comp, h, pl.ds(W - r0, SUB), :] = flip_rows(
                        sums[comp], sub
                    )

    def correlate(l, first):
        group = min(16, half)

        def step(i, carry):
            for g in range(group):
                r = first + i * group + g
                x = base + r
                for h in range(nh):
                    total = None
                    for part in range(2):
                        src = mirrored[part, h, pl.ds(W + 3 - x, SUB), :]
                        rec = fields[2 + part, h, pl.ds(x + 4, SUB), :]
                        total = src * rec if total is None else total + src * rec
                    terms[l, r, :, h * LANES : (h + 1) * LANES] = total
            return carry

        lax.fori_loop(0, half // group, step, 0)

    def pair_copy(l):
        return remote(
            terms.at[l, pl.ds((1 - core) * half, half)],
            pair_buf.at[l],
            pair_send.at[l],
            pair_recv.at[l],
            d,
            mate,
        )

    def ring_copy(l, s):
        other = lax.rem(chip + s, groups)
        return remote(
            terms.at[l, pl.ds(core * half + other * piece, piece)],
            ring_buf.at[l, s - 1],
            ring_send.at[l, s - 1],
            ring_recv.at[l, s - 1],
            d,
            2 * other + core,
        )

    def out_copy(l):
        return remote(
            done_buf.at[l],
            out.at[pl.ds(goal_part * piece, piece), 0],
            out_send.at[l],
            out_recv.at[goal_part],
            l,
            goal,
        )

    def pair_sum(l):
        pair_copy(l).wait_recv()
        for s in list(range(1, groups)) + [0]:
            at = lax.rem(chip + s, groups) * piece
            rows = pl.ds(core * half + at, piece)
            terms[l, rows] = terms[l, rows] + pair_buf[l, pl.ds(at, piece)]
            if s > 0:
                ring_copy(l, s).start()

    def ring_sum(l):
        total = terms[l, pl.ds(place, piece)]
        for s in range(1, groups):
            ring_copy(l, s).wait_recv()
            total = total + ring_buf[l, s - 1]
        mine = jnp.logical_and(l == d, goal == f)

        @pl.when(mine)
        def _():
            out[pl.ds(goal_part * piece, piece), 0] = total

        @pl.when(jnp.logical_not(mine))
        def _():
            done_buf[l] = total
            out_copy(l).start()

    def level(l, carry):
        for k in range(1, K):
            chebyshev(k)

        @pl.when(jnp.logical_and(l == 0, d > 0))
        def _():
            for copy in cls_copies:
                copy.start()

        @pl.when(l == 0)
        def _():
            pass_on(0)

        @pl.when(l > 0)
        def _():
            pair_sum(l - 1)

        classes_ready(l)
        combine(l)
        correlate(l, (1 - core) * half)
        pair_copy(l).start()
        correlate(l, core * half)

        @pl.when(l + 1 < nd)
        def _():
            pass_on(l + 1)

        @pl.when(l > 1)
        def _():
            ring_sum(l - 2)

        return carry

    lax.fori_loop(0, nd, level, 0)
    pair_sum(nd - 1)
    if nd >= 2:
        ring_sum(nd - 2)
    ring_sum(nd - 1)

    for copy in cls_copies:
        copy.wait_send()
    for l in range(nd):

        @pl.when(d != l)
        def _():
            forward(l).wait_send()

        pair_copy(l).wait_send()
        for s in range(1, groups):
            ring_copy(l, s).wait_send()

        @pl.when(jnp.logical_not(jnp.logical_and(l == d, goal == f)))
        def _():
            out_copy(l).wait_send()

    for part in range(out_parts):

        @pl.when(jnp.logical_not(is_mine(part)))
        def _():
            remote(
                done_buf.at[0],
                out.at[pl.ds(part * piece, piece), 0],
                out_send.at[0],
                out_recv.at[part],
                from_depth,
                giver(part),
            ).wait_recv()


def solution(mesh):
    nd, nf = mesh.shape["depth"], mesh.shape["freq"]

    def per_device(source, receiver, classes, coef_table, freq_list):
        rows_x, cols_y = source.shape[2], source.shape[3]
        K = coef_table.shape[3]
        rows_here = rows_x // nd
        reach = nd * (K - 1) + H // 2
        wide = -(-reach // SUB) * SUB
        W = min(rows_x, rows_here + 2 * wide)
        nh = cols_y // LANES
        groups = nf // 2
        piece = rows_here // nf
        rows_out = rows_x // nf
        cfg = dict(nd=nd, nf=nf, rows_x=rows_x, cols_y=cols_y, K=K, W=W)
        coef = jnp.transpose(coef_table, (1, 3, 2, 0))
        hbm = pl.BlockSpec(memory_space=pltpu.HBM)
        vmem = pl.BlockSpec(memory_space=pltpu.VMEM)
        dma = pltpu.SemaphoreType.DMA
        field = pltpu.VMEM((4, nh, W + 2 * SUB, LANES), jnp.float32)
        summed = pl.pallas_call(
            functools.partial(kernel, cfg),
            out_shape=pltpu.VMEM((rows_out, 1, H, cols_y), jnp.float32),
            in_specs=[hbm, hbm, hbm, vmem, pl.BlockSpec(memory_space=pltpu.SMEM)],
            out_specs=vmem,
            scratch_shapes=[
                pltpu.VMEM((2 * K, LANES), jnp.float32),
                field,
                pltpu.VMEM((2, nh, W + 2 * SUB, LANES), jnp.float32),
                pltpu.VMEM((nd, W, cols_y), jnp.int32),
                pltpu.VMEM((nd, rows_here, H, cols_y), jnp.float32),
                pltpu.VMEM((nd, rows_here // 2, H, cols_y), jnp.float32),
                pltpu.VMEM((nd, max(groups - 1, 1), piece, H, cols_y), jnp.float32),
                pltpu.VMEM((nd, piece, H, cols_y), jnp.float32),
                dma((4 * nh,)),
                dma,
                dma((nd,)),
                dma((nd,)),
                dma((nd,)),
                dma((nd,)),
                dma((nd,)),
                dma((nd,)),
                dma((nd, max(groups - 1, 1))),
                dma((nd, max(groups - 1, 1))),
                dma((nd,)),
                dma((rows_out // piece,)),
            ]
            + [field] * (K - 1),
            compiler_params=pltpu.CompilerParams(
                collective_id=0, has_side_effects=True, vmem_limit_bytes=62 * 1024 * 1024
            ),
        )(source, receiver, classes, coef, freq_list)
        return summed * float(nf) ** -0.5

    return jax.shard_map(
        per_device,
        mesh=mesh,
        in_specs=(
            P("freq", None, None, None),
            P("freq", None, None, None),
            P("depth", None, None),
            P(),
            P("freq"),
        ),
        out_specs=P("freq", "depth", None, None),
        check_vma=False,
    )
```

```python
import functools

import jax
import jax.numpy as jnp
from jax import lax
from jax.experimental import pallas as pl
from jax.experimental.pallas import tpu as pltpu
from jax.sharding import PartitionSpec as P

H = 8
LANES = 128
SUB = 8


def flip_rows(v, sub):
    v = pltpu.roll(v, 4, 0)
    v = jnp.where((sub & 2) == 0, pltpu.roll(v, 6, 0), pltpu.roll(v, 2, 0))
    return jnp.where((sub & 1) == 0, pltpu.roll(v, 7, 0), pltpu.roll(v, 1, 0))


def kernel(
    cfg,
    source,
    receiver,
    classes,
    coef,
    freq_row,
    out,
    tables,
    fields,
    mirrored,
    cls,
    terms,
    pair_buf,
    ring_buf,
    done_buf,
    load_sem,
    own_cls_sem,
    cls_send,
    cls_recv,
    fwd_send,
    fwd_recv,
    pair_send,
    pair_recv,
    ring_send,
    ring_recv,
    out_send,
    out_recv,
    *higher,
):
    nd, nf, rows_x, cols_y, K, W = (cfg[n] for n in ("nd", "nf", "rows_x", "cols_y", "K", "W"))
    nh = cols_y // LANES
    rows_here = rows_x // nd
    half = rows_here // 2
    groups = nf // 2
    piece = rows_here // nf
    rows_out = rows_x // nf
    owners = nf // nd
    out_parts = rows_out // piece
    wide = (W - rows_here) // 2
    cls_half = W // 2

    d = lax.axis_index("depth")
    f = lax.axis_index("freq")
    core = lax.rem(f, 2)
    chip = f // 2
    mate = f + 1 - 2 * core

    def window(depth):
        return pl.multiple_of(jnp.minimum(jnp.maximum(depth * rows_here - wide, 0), rows_x - W), SUB)

    start = window(d)
    base = pl.multiple_of(d * rows_here - start, SUB)

    def remote(src, dst, send, recv, dep, fre):
        return pltpu.make_async_remote_copy(
            src_ref=src,
            dst_ref=dst,
            send_sem=send,
            recv_sem=recv,
            device_id={"depth": dep, "freq": fre},
            device_id_type=pl.DeviceIdType.MESH,
        )

    place = core * half + chip * piece
    goal = d * owners + place // rows_out
    goal_part = lax.rem(place, rows_out) // piece
    from_depth = f // owners

    def giver(part):
        row = lax.rem(f, owners) * rows_out + part * piece
        return 2 * (lax.rem(row, half) // piece) + row // half

    def is_mine(part):
        return jnp.logical_and(from_depth == d, giver(part) == f)

    loads = []
    for comp in range(4):
        ref = source if comp < 2 else receiver
        for h in range(nh):
            loads.append(
                pltpu.make_async_copy(
                    ref.at[0, comp % 2, pl.ds(start, W), pl.ds(h * LANES, LANES)],
                    fields.at[comp, h, pl.ds(SUB, W), :],
                    load_sem.at[comp * nh + h],
                )
            )
            loads[-1].start()
    own_cls = pltpu.make_async_copy(classes.at[0, pl.ds(start, W)], cls.at[d], own_cls_sem)
    own_cls.start()

    barrier = pltpu.get_barrier_semaphore()

    def greet(dep, fre):
        pl.semaphore_signal(
            barrier,
            inc=1,
            device_id={"depth": dep, "freq": fre},
            device_id_type=pl.DeviceIdType.MESH,
        )

    for s in range(1, nd):
        greet(lax.rem(d + s, nd), f)
    greet(d, mate)
    for s in range(1, groups):
        greet(d, 2 * lax.rem(chip + s, groups) + core)
    for part in range(out_parts):

        @pl.when(jnp.logical_not(is_mine(part)))
        def _():
            greet(from_depth, giver(part))

    targets = (nd - 1) + 1 + (groups - 1) + nd
    pl.semaphore_wait(barrier, targets - jnp.where(goal == f, 1, 0))

    cls_rows = pl.multiple_of(core * cls_half, SUB)
    cls_copies = []
    for s in range(nd - 1, 0, -1):
        to = lax.rem(d + s, nd)
        src_row = pl.multiple_of(window(to) + cls_rows, SUB)
        copy = remote(
            classes.at[0, pl.ds(src_row, cls_half)],
            cls.at[d, pl.ds(cls_rows, cls_half)],
            cls_send.at[s - 1],
            cls_recv.at[d],
            to,
            f,
        )
        cls_copies.append(copy)

    @pl.when(d == 0)
    def _():
        for copy in cls_copies:
            copy.start()


    def forward(l):
        part = cls.at[l, pl.ds(cls_rows, cls_half)]
        return remote(part, part, fwd_send.at[l], fwd_recv.at[l], d, mate)

    def pass_on(l):
        @pl.when(d != l)
        def _():
            part = cls.at[l, pl.ds(cls_rows, cls_half)]
            remote(part, part, cls_send.at[0], cls_recv.at[l], d, mate).wait_recv()
            forward(l).start()

    def classes_ready(l):
        @pl.when(d != l)
        def _():
            forward(l).wait_recv()

        @pl.when(d == l)
        def _():
            own_cls.wait()

    held = (fields,) + higher
    row = freq_row[0]
    for k in range(K):
        for p in range(2):
            at = p * K + k
            tables[at : at + 1, 0 : coef.shape[3]] = coef[row, k, p : p + 1, :]
    zero = jnp.zeros((SUB, LANES), jnp.float32)
    for comp in range(4):
        for h in range(nh):
            for ref in held:
                ref[comp, h, 0:SUB, :] = zero
                ref[comp, h, W + SUB : W + 2 * SUB, :] = zero
            if comp < 2:
                mirrored[comp, h, 0:SUB, :] = zero
                mirrored[comp, h, W + SUB : W + 2 * SUB, :] = zero

    lane = lax.broadcasted_iota(jnp.int32, (SUB, LANES), 1)
    sub = lax.broadcasted_iota(jnp.int32, (SUB, LANES), 0)
    first_lane = lane == 0
    last_lane = lane == LANES - 1

    for copy in loads:
        copy.wait()

    def chebyshev(k):
        for r0 in range(0, W, SUB):
            for comp in range(4):
                twice, single, along, lefts, rights = [], [], [], [], []
                for h in range(nh):
                    v = held[k - 1][comp, h, pl.ds(r0 + SUB, SUB), :]
                    up = held[k - 1][comp, h, pl.ds(r0 + SUB - 1, SUB), :]
                    down = held[k - 1][comp, h, pl.ds(r0 + SUB + 1, SUB), :]
                    v2 = v + v
                    x_sum = up + down + v2
                    single.append(v)
                    twice.append(v2)
                    along.append(x_sum)
                    lefts.append(pltpu.roll(x_sum, 1, 1))
                    rights.append(pltpu.roll(x_sum, LANES - 1, 1))
                for h in range(nh):
                    left = jnp.where(first_lane, lefts[h - 1] if h > 0 else 0.0, lefts[h])
                    right = jnp.where(last_lane, rights[h + 1] if h + 1 < nh else 0.0, rights[h])
                    total = left + right + (along[h] + along[h])
                    if k == 1:
                        result = 0.125 * total - single[h]
                    else:
                        earlier = held[k - 2][comp, h, pl.ds(r0 + SUB, SUB), :]
                        result = 0.25 * total - (twice[h] + earlier)
                    held[k][comp, h, pl.ds(r0 + SUB, SUB), :] = result

    def combine(l):
        for r0 in range(0, W, SUB):
            rows = pl.ds(r0 + SUB, SUB)
            for h in range(nh):
                which = cls[l, pl.ds(r0, SUB), h * LANES : (h + 1) * LANES]
                sums = None
                for k in range(K):
                    cr, ci = (
                        jnp.take_along_axis(
                            jnp.broadcast_to(tables[p * K + k : p * K + k + 1, :], (SUB, LANES)),
                            which,
                            axis=1,
                            mode="promise_in_bounds",
                        )
                        for p in range(2)
                    )
                    sr, si, rr, ri = (held[k][comp, h, rows, :] for comp in range(4))
                    new = (
                        cr * sr + ci * si,
                        cr * si - ci * sr,
                        cr * rr - ci * ri,
                        cr * ri + ci * rr,
                    )
                    sums = new if sums is None else tuple(a + b for a, b in zip(sums, new))
                for comp in range(4):
                    fields[comp, h, rows, :] = sums[comp]
                for comp in range(2):
                    mirrored[comp, h, pl.ds(W - r0, SUB), :] = flip_rows(
                        sums[comp], sub
                    )

    def correlate(l, first):
        group = min(16, half)

        def step(i, carry):
            for g in range(group):
                r = first + i * group + g
                x = base + r
                for h in range(nh):
                    total = None
                    for part in range(2):
                        src = mirrored[part, h, pl.ds(W + 3 - x, SUB), :]
                        rec = fields[2 + part, h, pl.ds(x + 4, SUB), :]
                        total = src * rec if total is None else total + src * rec
                    terms[l, r, :, h * LANES : (h + 1) * LANES] = total
            return carry

        lax.fori_loop(0, half // group, step, 0)

    def pair_copy(l):
        return remote(
            terms.at[l, pl.ds((1 - core) * half, half)],
            pair_buf.at[l],
            pair_send.at[l],
            pair_recv.at[l],
            d,
            mate,
        )

    def ring_copy(l, s):
        other = lax.rem(chip + s, groups)
        return remote(
            terms.at[l, pl.ds(core * half + other * piece, piece)],
            ring_buf.at[l, s - 1],
            ring_send.at[l, s - 1],
            ring_recv.at[l, s - 1],
            d,
            2 * other + core,
        )

    def out_copy(l):
        return remote(
            done_buf.at[l],
            out.at[pl.ds(goal_part * piece, piece), 0],
            out_send.at[l],
            out_recv.at[goal_part],
            l,
            goal,
        )

    def pair_sum(l):
        pair_copy(l).wait_recv()
        for s in list(range(1, groups)) + [0]:
            at = lax.rem(chip + s, groups) * piece
            rows = pl.ds(core * half + at, piece)
            terms[l, rows] = terms[l, rows] + pair_buf[l, pl.ds(at, piece)]
            if s > 0:
                ring_copy(l, s).start()

    def ring_sum(l):
        total = terms[l, pl.ds(place, piece)]
        for s in range(1, groups):
            ring_copy(l, s).wait_recv()
            total = total + ring_buf[l, s - 1]
        mine = jnp.logical_and(l == d, goal == f)

        @pl.when(mine)
        def _():
            out[pl.ds(goal_part * piece, piece), 0] = total

        @pl.when(jnp.logical_not(mine))
        def _():
            done_buf[l] = total
            out_copy(l).start()

    def level(l, carry):
        early = min(3, K)
        for k in range(1, early):
            chebyshev(k)

        @pl.when(l > 0)
        def _():
            pair_sum(l - 1)

        @pl.when(jnp.logical_and(l == 0, d > 0))
        def _():
            for copy in cls_copies:
                copy.start()

        for k in range(early, K):
            chebyshev(k)

        @pl.when(l == 0)
        def _():
            pass_on(0)

        classes_ready(l)
        combine(l)
        correlate(l, (1 - core) * half)
        pair_copy(l).start()
        correlate(l, core * half)

        @pl.when(l + 1 < nd)
        def _():
            pass_on(l + 1)

        @pl.when(l > 1)
        def _():
            ring_sum(l - 2)

        return carry

    lax.fori_loop(0, nd, level, 0)
    pair_sum(nd - 1)
    if nd >= 2:
        ring_sum(nd - 2)
    ring_sum(nd - 1)

    for copy in cls_copies:
        copy.wait_send()
    for l in range(nd):

        @pl.when(d != l)
        def _():
            forward(l).wait_send()

        pair_copy(l).wait_send()
        for s in range(1, groups):
            ring_copy(l, s).wait_send()

        @pl.when(jnp.logical_not(jnp.logical_and(l == d, goal == f)))
        def _():
            out_copy(l).wait_send()

    for part in range(out_parts):

        @pl.when(jnp.logical_not(is_mine(part)))
        def _():
            remote(
                done_buf.at[0],
                out.at[pl.ds(part * piece, piece), 0],
                out_send.at[0],
                out_recv.at[part],
                from_depth,
                giver(part),
            ).wait_recv()


def solution(mesh):
    nd, nf = mesh.shape["depth"], mesh.shape["freq"]

    def per_device(source, receiver, classes, coef_table, freq_list):
        rows_x, cols_y = source.shape[2], source.shape[3]
        K = coef_table.shape[3]
        rows_here = rows_x // nd
        reach = nd * (K - 1) + H // 2
        wide = -(-reach // SUB) * SUB
        W = min(rows_x, rows_here + 2 * wide)
        nh = cols_y // LANES
        groups = nf // 2
        piece = rows_here // nf
        rows_out = rows_x // nf
        cfg = dict(nd=nd, nf=nf, rows_x=rows_x, cols_y=cols_y, K=K, W=W)
        coef = jnp.transpose(coef_table, (1, 3, 2, 0))
        hbm = pl.BlockSpec(memory_space=pltpu.HBM)
        vmem = pl.BlockSpec(memory_space=pltpu.VMEM)
        dma = pltpu.SemaphoreType.DMA
        field = pltpu.VMEM((4, nh, W + 2 * SUB, LANES), jnp.float32)
        summed = pl.pallas_call(
            functools.partial(kernel, cfg),
            out_shape=pltpu.VMEM((rows_out, 1, H, cols_y), jnp.float32),
            in_specs=[hbm, hbm, hbm, vmem, pl.BlockSpec(memory_space=pltpu.SMEM)],
            out_specs=vmem,
            scratch_shapes=[
                pltpu.VMEM((2 * K, LANES), jnp.float32),
                field,
                pltpu.VMEM((2, nh, W + 2 * SUB, LANES), jnp.float32),
                pltpu.VMEM((nd, W, cols_y), jnp.int32),
                pltpu.VMEM((nd, rows_here, H, cols_y), jnp.float32),
                pltpu.VMEM((nd, rows_here // 2, H, cols_y), jnp.float32),
                pltpu.VMEM((nd, max(groups - 1, 1), piece, H, cols_y), jnp.float32),
                pltpu.VMEM((nd, piece, H, cols_y), jnp.float32),
                dma((4 * nh,)),
                dma,
                dma((nd,)),
                dma((nd,)),
                dma((nd,)),
                dma((nd,)),
                dma((nd,)),
                dma((nd,)),
                dma((nd, max(groups - 1, 1))),
                dma((nd, max(groups - 1, 1))),
                dma((nd,)),
                dma((rows_out // piece,)),
            ]
            + [field] * (K - 1),
            compiler_params=pltpu.CompilerParams(
                collective_id=0, has_side_effects=True, vmem_limit_bytes=62 * 1024 * 1024
            ),
        )(source, receiver, classes, coef, freq_list)
        return summed * float(nf) ** -0.5

    return jax.shard_map(
        per_device,
        mesh=mesh,
        in_specs=(
            P("freq", None, None, None),
            P("freq", None, None, None),
            P("depth", None, None),
            P(),
            P("freq"),
        ),
        out_specs=P("freq", "depth", None, None),
        check_vma=False,
    )
```

```python
import functools

import jax
import jax.numpy as jnp
from jax import lax
from jax.experimental import pallas as pl
from jax.experimental.pallas import tpu as pltpu
from jax.sharding import PartitionSpec as P

H = 8
LANES = 128
SUB = 8


def flip_rows(v, sub):
    v = pltpu.roll(v, 4, 0)
    v = jnp.where((sub & 2) == 0, pltpu.roll(v, 6, 0), pltpu.roll(v, 2, 0))
    return jnp.where((sub & 1) == 0, pltpu.roll(v, 7, 0), pltpu.roll(v, 1, 0))


def kernel(
    cfg,
    source,
    receiver,
    classes,
    coef,
    freq_row,
    out,
    tables,
    fields,
    mirrored,
    cls,
    terms,
    pair_buf,
    ring_buf,
    done_buf,
    load_sem,
    own_cls_sem,
    cls_send,
    cls_recv,
    fwd_send,
    fwd_recv,
    pair_send,
    pair_recv,
    ring_send,
    ring_recv,
    out_send,
    out_recv,
    *higher,
):
    nd, nf, rows_x, cols_y, K, W = (cfg[n] for n in ("nd", "nf", "rows_x", "cols_y", "K", "W"))
    nh = cols_y // LANES
    rows_here = rows_x // nd
    half = rows_here // 2
    groups = nf // 2
    piece = rows_here // nf
    rows_out = rows_x // nf
    owners = nf // nd
    out_parts = rows_out // piece
    wide = (W - rows_here) // 2
    cls_half = W // 2

    d = lax.axis_index("depth")
    f = lax.axis_index("freq")
    core = lax.rem(f, 2)
    chip = f // 2
    mate = f + 1 - 2 * core

    def window(depth):
        return pl.multiple_of(jnp.minimum(jnp.maximum(depth * rows_here - wide, 0), rows_x - W), SUB)

    start = window(d)
    base = pl.multiple_of(d * rows_here - start, SUB)

    def remote(src, dst, send, recv, dep, fre):
        return pltpu.make_async_remote_copy(
            src_ref=src,
            dst_ref=dst,
            send_sem=send,
            recv_sem=recv,
            device_id={"depth": dep, "freq": fre},
            device_id_type=pl.DeviceIdType.MESH,
        )

    place = core * half + chip * piece
    goal = d * owners + place // rows_out
    goal_part = lax.rem(place, rows_out) // piece
    from_depth = f // owners

    def giver(part):
        row = lax.rem(f, owners) * rows_out + part * piece
        return 2 * (lax.rem(row, half) // piece) + row // half

    def is_mine(part):
        return jnp.logical_and(from_depth == d, giver(part) == f)

    loads = []
    for comp in range(4):
        ref = source if comp < 2 else receiver
        for h in range(nh):
            loads.append(
                pltpu.make_async_copy(
                    ref.at[0, comp % 2, pl.ds(start, W), pl.ds(h * LANES, LANES)],
                    fields.at[comp, h, pl.ds(SUB, W), :],
                    load_sem.at[comp * nh + h],
                )
            )
            loads[-1].start()
    own_cls = pltpu.make_async_copy(classes.at[0, pl.ds(start, W)], cls.at[d], own_cls_sem)
    own_cls.start()

    barrier = pltpu.get_barrier_semaphore()

    def greet(dep, fre):
        pl.semaphore_signal(
            barrier,
            inc=1,
            device_id={"depth": dep, "freq": fre},
            device_id_type=pl.DeviceIdType.MESH,
        )

    for s in range(1, nd):
        greet(lax.rem(d + s, nd), f)
    greet(d, mate)
    for s in range(1, groups):
        greet(d, 2 * lax.rem(chip + s, groups) + core)
    for part in range(out_parts):

        @pl.when(jnp.logical_not(is_mine(part)))
        def _():
            greet(from_depth, giver(part))

    targets = (nd - 1) + 1 + (groups - 1) + nd
    pl.semaphore_wait(barrier, targets - jnp.where(goal == f, 1, 0))

    cls_rows = pl.multiple_of(core * cls_half, SUB)
    cls_copies = []
    for s in range(nd - 1, 0, -1):
        to = lax.rem(d + s, nd)
        src_row = pl.multiple_of(window(to) + cls_rows, SUB)
        copy = remote(
            classes.at[0, pl.ds(src_row, cls_half)],
            cls.at[d, pl.ds(cls_rows, cls_half)],
            cls_send.at[s - 1],
            cls_recv.at[d],
            to,
            f,
        )
        cls_copies.append(copy)

    @pl.when(d == 0)
    def _():
        for copy in cls_copies:
            copy.start()


    def forward(l):
        part = cls.at[l, pl.ds(cls_rows, cls_half)]
        return remote(part, part, fwd_send.at[l], fwd_recv.at[l], d, mate)

    def pass_on(l):
        @pl.when(d != l)
        def _():
            part = cls.at[l, pl.ds(cls_rows, cls_half)]
            remote(part, part, cls_send.at[0], cls_recv.at[l], d, mate).wait_recv()
            forward(l).start()

    def classes_ready(l):
        @pl.when(d != l)
        def _():
            forward(l).wait_recv()

        @pl.when(d == l)
        def _():
            own_cls.wait()

    held = (fields,) + higher
    row = freq_row[0]
    for k in range(K):
        for p in range(2):
            at = p * K + k
            tables[at : at + 1, 0 : coef.shape[3]] = coef[row, k, p : p + 1, :]
    zero = jnp.zeros((SUB, LANES), jnp.float32)
    for comp in range(4):
        for h in range(nh):
            for ref in held:
                ref[comp, h, 0:SUB, :] = zero
                ref[comp, h, W + SUB : W + 2 * SUB, :] = zero
            if comp < 2:
                mirrored[comp, h, 0:SUB, :] = zero
                mirrored[comp, h, W + SUB : W + 2 * SUB, :] = zero

    lane = lax.broadcasted_iota(jnp.int32, (SUB, LANES), 1)
    sub = lax.broadcasted_iota(jnp.int32, (SUB, LANES), 0)
    first_lane = lane == 0
    last_lane = lane == LANES - 1

    for copy in loads:
        copy.wait()

    def chebyshev(k):
        for r0 in range(0, W, SUB):
            for comp in range(4):
                twice, single, along, lefts, rights = [], [], [], [], []
                for h in range(nh):
                    v = held[k - 1][comp, h, pl.ds(r0 + SUB, SUB), :]
                    up = held[k - 1][comp, h, pl.ds(r0 + SUB - 1, SUB), :]
                    down = held[k - 1][comp, h, pl.ds(r0 + SUB + 1, SUB), :]
                    v2 = v + v
                    x_sum = up + down + v2
                    single.append(v)
                    twice.append(v2)
                    along.append(x_sum)
                    lefts.append(pltpu.roll(x_sum, 1, 1))
                    rights.append(pltpu.roll(x_sum, LANES - 1, 1))
                for h in range(nh):
                    left = jnp.where(first_lane, lefts[h - 1] if h > 0 else 0.0, lefts[h])
                    right = jnp.where(last_lane, rights[h + 1] if h + 1 < nh else 0.0, rights[h])
                    total = left + right + (along[h] + along[h])
                    if k == 1:
                        result = 0.125 * total - single[h]
                    else:
                        earlier = held[k - 2][comp, h, pl.ds(r0 + SUB, SUB), :]
                        result = 0.25 * total - (twice[h] + earlier)
                    held[k][comp, h, pl.ds(r0 + SUB, SUB), :] = result

    def combine(l):
        for r0 in range(0, W, SUB):
            rows = pl.ds(r0 + SUB, SUB)
            for h in range(nh):
                which = cls[l, pl.ds(r0, SUB), h * LANES : (h + 1) * LANES]
                sums = None
                for k in range(K):
                    cr, ci = (
                        jnp.take_along_axis(
                            jnp.broadcast_to(tables[p * K + k : p * K + k + 1, :], (SUB, LANES)),
                            which,
                            axis=1,
                            mode="promise_in_bounds",
                        )
                        for p in range(2)
                    )
                    sr, si, rr, ri = (held[k][comp, h, rows, :] for comp in range(4))
                    new = (
                        cr * sr + ci * si,
                        cr * si - ci * sr,
                        cr * rr - ci * ri,
                        cr * ri + ci * rr,
                    )
                    sums = new if sums is None else tuple(a + b for a, b in zip(sums, new))
                for comp in range(4):
                    fields[comp, h, rows, :] = sums[comp]
                for comp in range(2):
                    mirrored[comp, h, pl.ds(W - r0, SUB), :] = flip_rows(
                        sums[comp], sub
                    )

    def correlate(l, first):
        group = min(32, half)

        def step(i, carry):
            for g in range(group):
                r = first + i * group + g
                x = base + r
                for h in range(nh):
                    total = None
                    for part in range(2):
                        src = mirrored[part, h, pl.ds(W + 3 - x, SUB), :]
                        rec = fields[2 + part, h, pl.ds(x + 4, SUB), :]
                        total = src * rec if total is None else total + src * rec
                    terms[l, r, :, h * LANES : (h + 1) * LANES] = total
            return carry

        lax.fori_loop(0, half // group, step, 0)

    def pair_copy(l):
        return remote(
            terms.at[l, pl.ds((1 - core) * half, half)],
            pair_buf.at[l],
            pair_send.at[l],
            pair_recv.at[l],
            d,
            mate,
        )

    def ring_copy(l, s):
        other = lax.rem(chip + s, groups)
        return remote(
            terms.at[l, pl.ds(core * half + other * piece, piece)],
            ring_buf.at[l, s - 1],
            ring_send.at[l, s - 1],
            ring_recv.at[l, s - 1],
            d,
            2 * other + core,
        )

    def out_copy(l):
        return remote(
            done_buf.at[l],
            out.at[pl.ds(goal_part * piece, piece), 0],
            out_send.at[l],
            out_recv.at[goal_part],
            l,
            goal,
        )

    def pair_sum(l):
        pair_copy(l).wait_recv()
        for s in list(range(1, groups)) + [0]:
            at = lax.rem(chip + s, groups) * piece
            rows = pl.ds(core * half + at, piece)
            terms[l, rows] = terms[l, rows] + pair_buf[l, pl.ds(at, piece)]
            if s > 0:
                ring_copy(l, s).start()

    def ring_sum(l):
        total = terms[l, pl.ds(place, piece)]
        for s in range(1, groups):
            ring_copy(l, s).wait_recv()
            total = total + ring_buf[l, s - 1]
        mine = jnp.logical_and(l == d, goal == f)

        @pl.when(mine)
        def _():
            out[pl.ds(goal_part * piece, piece), 0] = total

        @pl.when(jnp.logical_not(mine))
        def _():
            done_buf[l] = total
            out_copy(l).start()

    def level(l, carry):
        early = min(3, K)
        for k in range(1, early):
            chebyshev(k)

        @pl.when(l > 0)
        def _():
            pair_sum(l - 1)

        @pl.when(jnp.logical_and(l == 0, d > 0))
        def _():
            for copy in cls_copies:
                copy.start()

        for k in range(early, K):
            chebyshev(k)

        @pl.when(l == 0)
        def _():
            pass_on(0)

        classes_ready(l)
        combine(l)
        correlate(l, (1 - core) * half)
        pair_copy(l).start()
        correlate(l, core * half)

        @pl.when(l + 1 < nd)
        def _():
            pass_on(l + 1)

        @pl.when(l > 1)
        def _():
            ring_sum(l - 2)

        return carry

    lax.fori_loop(0, nd, level, 0)
    pair_sum(nd - 1)
    if nd >= 2:
        ring_sum(nd - 2)
    ring_sum(nd - 1)

    for copy in cls_copies:
        copy.wait_send()
    for l in range(nd):

        @pl.when(d != l)
        def _():
            forward(l).wait_send()

        pair_copy(l).wait_send()
        for s in range(1, groups):
            ring_copy(l, s).wait_send()

        @pl.when(jnp.logical_not(jnp.logical_and(l == d, goal == f)))
        def _():
            out_copy(l).wait_send()

    for part in range(out_parts):

        @pl.when(jnp.logical_not(is_mine(part)))
        def _():
            remote(
                done_buf.at[0],
                out.at[pl.ds(part * piece, piece), 0],
                out_send.at[0],
                out_recv.at[part],
                from_depth,
                giver(part),
            ).wait_recv()


def solution(mesh):
    nd, nf = mesh.shape["depth"], mesh.shape["freq"]

    def per_device(source, receiver, classes, coef_table, freq_list):
        rows_x, cols_y = source.shape[2], source.shape[3]
        K = coef_table.shape[3]
        rows_here = rows_x // nd
        reach = nd * (K - 1) + H // 2
        wide = -(-reach // SUB) * SUB
        W = min(rows_x, rows_here + 2 * wide)
        nh = cols_y // LANES
        groups = nf // 2
        piece = rows_here // nf
        rows_out = rows_x // nf
        cfg = dict(nd=nd, nf=nf, rows_x=rows_x, cols_y=cols_y, K=K, W=W)
        coef = jnp.transpose(coef_table, (1, 3, 2, 0))
        hbm = pl.BlockSpec(memory_space=pltpu.HBM)
        vmem = pl.BlockSpec(memory_space=pltpu.VMEM)
        dma = pltpu.SemaphoreType.DMA
        field = pltpu.VMEM((4, nh, W + 2 * SUB, LANES), jnp.float32)
        summed = pl.pallas_call(
            functools.partial(kernel, cfg),
            out_shape=pltpu.VMEM((rows_out, 1, H, cols_y), jnp.float32),
            in_specs=[hbm, hbm, hbm, vmem, pl.BlockSpec(memory_space=pltpu.SMEM)],
            out_specs=vmem,
            scratch_shapes=[
                pltpu.VMEM((2 * K, LANES), jnp.float32),
                field,
                pltpu.VMEM((2, nh, W + 2 * SUB, LANES), jnp.float32),
                pltpu.VMEM((nd, W, cols_y), jnp.int32),
                pltpu.VMEM((nd, rows_here, H, cols_y), jnp.float32),
                pltpu.VMEM((nd, rows_here // 2, H, cols_y), jnp.float32),
                pltpu.VMEM((nd, max(groups - 1, 1), piece, H, cols_y), jnp.float32),
                pltpu.VMEM((nd, piece, H, cols_y), jnp.float32),
                dma((4 * nh,)),
                dma,
                dma((nd,)),
                dma((nd,)),
                dma((nd,)),
                dma((nd,)),
                dma((nd,)),
                dma((nd,)),
                dma((nd, max(groups - 1, 1))),
                dma((nd, max(groups - 1, 1))),
                dma((nd,)),
                dma((rows_out // piece,)),
            ]
            + [field] * (K - 1),
            compiler_params=pltpu.CompilerParams(
                collective_id=0, has_side_effects=True, vmem_limit_bytes=62 * 1024 * 1024
            ),
        )(source, receiver, classes, coef, freq_list)
        return summed * float(nf) ** -0.5

    return jax.shard_map(
        per_device,
        mesh=mesh,
        in_specs=(
            P("freq", None, None, None),
            P("freq", None, None, None),
            P("depth", None, None),
            P(),
            P("freq"),
        ),
        out_specs=P("freq", "depth", None, None),
        check_vma=False,
    )
```
